256 devices in a mesh: replica: 32 (over x_lo, z, core), tensor: 8 (over x_hi, y).
Axes of the slice: x: 4 (x_hi: 2, x_lo: 2; x = x_hi * 2 + x_lo), y: 4, z: 8, core: 2. Of those that a mesh axis runs over, the one named last changes fastest.
Arguments:
- context: bfloat16 [32, 2048, 1792], P('replica', None, 'tensor'), may hold values from -6 to 6
- out_grad: bfloat16 [32, 2048, 3584], P('replica', 'tensor'), may hold values from -6 to 6
- params: float32 [32, 1792, 3584], P('replica', 'tensor'), may hold values from -6 to 6
- momentum: bfloat16 [32, 1792, 3584], P('replica', 'tensor'), may hold values from -180 to 180
Outputs:
- mixed_params: float32 [32, 1792, 3584], P('replica', 'tensor')
- mixed_momentum: bfloat16 [32, 1792, 3584], P('replica', 'tensor')
The draws below stay inside these ranges and needn't reach their ends.
All inputs are finite; a program needn't handle non-finite values.
Results may differ from the reference program's by a relative error of at most 0.0052.
Values may be sent and summed in bfloat16 or wider, within the bound.
No kernel may reach another device: no remote copies, remote signals or barrier semaphores. Data moves between devices by JAX's collectives and lax.ppermute only.
A program may use at most 128 MiB of HBM per device.

```python
import jax
import jax.numpy as jnp
from jax import lax

D = 3584
TOK = 2048
ROWS = 1792
REPS = 32


def steps_of(stream_key, shape, shards, smallest, largest):
    factor_of, own = 1.0, jax.random.fold_in(stream_key, 6)
    for dim, shards_of in shards:
        draws = jnp.exp(jax.random.uniform(jax.random.fold_in(own, dim), (shards_of,), jnp.float32, smallest / len(shards), largest / len(shards)))
        factor_of = factor_of * jnp.repeat(draws, shape[dim] // shards_of).reshape([-1 if axis == dim else 1 for axis in range(len(shape))])
    return factor_of


def noise(rng, dims, spread, most, pieces=(), dtype=jnp.bfloat16):
    entries = spread * jax.random.normal(rng, dims, jnp.float32)
    if pieces:
        entries = entries * steps_of(rng, dims, pieces, -0.22, 0.18)
    return jnp.clip(entries, -most, most).astype(dtype)


def setup_inputs(seed: int = 0) -> dict:
    key_list = jax.random.split(jax.random.key(seed), 5)
    context = noise(key_list[0], (REPS, TOK, ROWS), 1.0, 6.0, ((0, 32), (2, 8)))
    out_grad = noise(key_list[1], (REPS, TOK, D), 1.0, 6.0, ((0, 32), (1, 8)))
    params = noise(key_list[2], (REPS, ROWS, D), 1.0, 6.0, ((0, 32), (1, 8)), jnp.float32)
    momentum = noise(key_list[3], (REPS, ROWS, D), 30.0, 180.0, ((0, 32), (1, 8)))
    return {"context": context, "out_grad": out_grad, "params": params, "momentum": momentum}


learn_rate = 0.01
beta_decay = 0.9

def rounded(values):
    return lax.optimization_barrier(values.astype(jnp.bfloat16)).astype(jnp.float32)

def blend(own, sent, stride):
    return (own + jnp.roll(sent, stride, 0) + jnp.roll(sent, -stride, 0)) / 3.0

def reference(context, out_grad, params, momentum):

    def one_grad(pair):
        return jnp.dot(pair[0].T, pair[1], preferred_element_type=jnp.float32)
    grad = lax.map(one_grad, (context, out_grad))
    velocity = beta_decay * momentum.astype(jnp.float32) + grad
    stepped = params - learn_rate * velocity
    params_one = blend(stepped, rounded(stepped), 1)
    velocity_one = blend(velocity, rounded(velocity), 1)
    params_two = blend(params_one, rounded(params_one), 2)
    velocity_two = blend(velocity_one, rounded(velocity_one), 2)
    return (params_two, velocity_two.astype(jnp.bfloat16))
```

```python
import functools

import jax
import jax.numpy as jnp
from jax import lax
from jax.experimental import pallas as pl
from jax.experimental.pallas import tpu as pltpu
from jax.sharding import PartitionSpec as P

learn_rate = 0.01
beta_decay = 0.9

BOTH = ("replica", "tensor")
TILE = 256
CHUNKS = ((0, 4), (4, 3))
HALF_TILES = 7
bf16, f32 = jnp.bfloat16, jnp.float32


def passed_along(value, axis, steps):
    count = lax.axis_size(axis)
    pairs = [(source, (source + steps) % count) for source in range(count)]
    return lax.ppermute(value, axis, pairs)


def swap_half(value):
    return lax.ppermute(value, "tensor", [(t, t ^ 4) for t in range(8)])


def ring_step(value):
    pairs = []
    for r in range(32):
        way = 1 if r % 2 == 0 else -1
        for t in range(8):
            pairs.append((r * 8 + t, r * 8 + (t & 4) + ((t + way) & 3)))
    return lax.ppermute(value, BOTH, pairs)


def grad_kernel(s_ref, own_ref, oth_ref, g0, g1, g2, g3, mom_ref, v32_ref, v16_ref, goth_ref):
    acc_own = jnp.zeros(goth_ref.shape, f32)
    acc_oth = jnp.zeros(goth_ref.shape, f32)
    for step, blocks in enumerate((g0, g1, g2, g3)):
        for part in range(2):
            tokens = pl.ds(pl.multiple_of(s_ref[1 + 2 * step + part] * 256, 256), 256)
            block = blocks[part * 256 : (part + 1) * 256, :]
            acc_own += jnp.dot(own_ref[:, tokens], block, preferred_element_type=f32)
            acc_oth += jnp.dot(oth_ref[:, tokens], block, preferred_element_type=f32)
    velocity = beta_decay * mom_ref[...].astype(f32) + acc_own
    v32_ref[0] = velocity
    v16_ref[0] = velocity.astype(bf16)
    goth_ref[...] = acc_oth.astype(bf16)


def grads(scalars, own, oth, blocks, momentum, first, tiles):
    rows, tokens = own.shape
    cols = tiles * TILE
    whole = pl.BlockSpec((rows, tokens), lambda j, s: (0, 0))
    block = pl.BlockSpec((512, TILE), lambda j, s: (0, j))
    mom = pl.BlockSpec((rows, TILE), lambda j, s: (0, s[0] * HALF_TILES + first + j))
    half = pl.BlockSpec((1, rows, TILE), lambda j, s: (0, 0, j))
    return pl.pallas_call(
        grad_kernel,
        grid_spec=pltpu.PrefetchScalarGridSpec(
            num_scalar_prefetch=1,
            grid=(tiles,),
            in_specs=[whole, whole, block, block, block, block, mom],
            out_specs=[half, half, pl.BlockSpec((rows, TILE), lambda j, s: (0, j))],
        ),
        out_shape=[
            jax.ShapeDtypeStruct((2, rows, cols), f32),
            jax.ShapeDtypeStruct((2, rows, cols), bf16),
            jax.ShapeDtypeStruct((rows, cols), bf16),
        ],
        cost_estimate=pl.CostEstimate(
            flops=4 * rows * tokens * cols, bytes_accessed=2 * tokens * cols + 4 * rows * tokens + 10 * rows * cols, transcendentals=0
        ),
        name="grads",
    )(scalars, own, oth, *blocks, momentum)


def other_kernel(s_ref, v32_in, v16_in, grad_ref, mom_ref, v32_ref, v16_ref):
    velocity = beta_decay * mom_ref[...].astype(f32) + grad_ref[...].astype(f32)
    v32_ref[0] = velocity
    v16_ref[0] = velocity.astype(bf16)


def other_half(scalars, v32, v16, grad, momentum, first, tiles):
    rows = grad.shape[0]
    anywhere = pl.BlockSpec(memory_space=pl.ANY)
    half = pl.BlockSpec((1, rows, TILE), lambda j, s: (1, 0, j))
    return pl.pallas_call(
        other_kernel,
        grid_spec=pltpu.PrefetchScalarGridSpec(
            num_scalar_prefetch=1,
            grid=(tiles,),
            in_specs=[
                anywhere,
                anywhere,
                pl.BlockSpec((rows, TILE), lambda j, s: (0, j)),
                pl.BlockSpec((rows, TILE), lambda j, s: (0, (1 - s[0]) * HALF_TILES + first + j)),
            ],
            out_specs=[half, half],
        ),
        out_shape=[jax.ShapeDtypeStruct(v32.shape, f32), jax.ShapeDtypeStruct(v16.shape, bf16)],
        input_output_aliases={1: 0, 2: 1},
        cost_estimate=pl.CostEstimate(flops=2 * grad.size, bytes_accessed=10 * grad.size, transcendentals=0),
        name="other_half",
    )(scalars, v32, v16, grad, momentum)


def final_kernel(s_ref, *refs):
    v1, vb, va, p1, pb, pa, out_p, out_m = refs[-8:]
    velocity = (v1[0] + vb[0].astype(f32) + va[0].astype(f32)) / 3.0
    params = (p1[...] + pb[...].astype(f32) + pa[...].astype(f32)) / 3.0
    out_p[...] = params - learn_rate * velocity
    out_m[...] = velocity.astype(bf16)


def finals(scalars, before, v1, vb, va, p1, pb, pa, first, tiles):
    rows, width = p1.shape
    rel = pl.BlockSpec((1, rows, TILE), lambda half, j, s: (half, 0, j))
    placed = pl.BlockSpec((rows, TILE), lambda half, j, s: (0, (s[0] + half - 2 * s[0] * half) * HALF_TILES + first + j))
    return pl.pallas_call(
        final_kernel,
        grid_spec=pltpu.PrefetchScalarGridSpec(
            num_scalar_prefetch=1,
            grid=(2, tiles),
            in_specs=[pl.BlockSpec(memory_space=pl.ANY)] * len(before) + [rel, rel, rel, placed, placed, placed],
            out_specs=[placed, placed],
        ),
        out_shape=[jax.ShapeDtypeStruct((rows, width), f32), jax.ShapeDtypeStruct((rows, width), bf16)],
        input_output_aliases={1: 0, 2: 1} if before else {},
        cost_estimate=pl.CostEstimate(flops=10 * v1.size, bytes_accessed=22 * v1.size, transcendentals=0),
        name="finals",
    )(scalars, *before, v1, vb, va, p1, pb, pa)


def body(context, out_grad, params, momentum):
    r, t = lax.axis_index("replica"), lax.axis_index("tensor")
    h, y = t // 4, t % 4
    way = 1 - 2 * (r % 2)
    order = [h]
    for step in range(4):
        spot = (y - way * step) % 4
        order += [h * 4 + spot, (1 - h) * 4 + spot]
    scalars = jnp.stack(order).astype(jnp.int32)

    own_ctx = context[0].T
    cot = out_grad[0]
    mom = momentum[0]
    param = params[0]
    width = cot.shape[1]
    half_width = width // 2

    p_sent = param.astype(bf16)
    p_low, p_up = passed_along(p_sent, "replica", 1), passed_along(p_sent, "replica", -1)
    p1 = (param + p_low.astype(f32) + p_up.astype(f32)) / 3.0
    p1_sent = p1.astype(bf16)
    p2_low, p2_up = passed_along(p1_sent, "replica", 2), passed_along(p1_sent, "replica", -2)

    oth_ctx = swap_half(own_ctx)
    done = ()
    for first, tiles in CHUNKS:
        lo, hi = first * TILE, (first + tiles) * TILE
        left, right = cot[:, lo:hi], cot[:, half_width + lo : half_width + hi]
        keep = jnp.where(h == 0, left, right)
        give = jnp.where(h == 0, right, left)
        block = jnp.concatenate([keep, swap_half(give)], 0)
        blocks = [block]
        for _ in range(3):
            blocks.append(ring_step(blocks[-1]))
        v32, v16, g_oth = grads(scalars, own_ctx, oth_ctx, blocks, mom, first, tiles)
        v32, v16 = other_half(scalars, v32, v16, swap_half(g_oth), mom, first, tiles)
        low, up = passed_along(v16, "replica", 1), passed_along(v16, "replica", -1)
        v1 = (v32 + low.astype(f32) + up.astype(f32)) / 3.0
        v1_sent = v1.astype(bf16)
        low2, up2 = passed_along(v1_sent, "replica", 2), passed_along(v1_sent, "replica", -2)
        done = finals(scalars, done, v1, low2, up2, p1, p2_low, p2_up, first, tiles)
    return (done[0][None], done[1][None])


def solution(mesh):
    return jax.shard_map(
        body,
        mesh=mesh,
        in_specs=(
            P("replica", None, "tensor"),
            P("replica", "tensor", None),
            P("replica", "tensor", None),
            P("replica", "tensor", None),
        ),
        out_specs=(P("replica", "tensor", None), P("replica", "tensor", None)),
        check_vma=False,
    )
```

```python
import jax
import jax.numpy as jnp
from jax import lax
from jax.sharding import PartitionSpec as P

learn_rate = 0.01
beta_decay = 0.9

BOTH = ("replica", "tensor")
CUTS = ((0, 2048), (2048, 3584))
bf16, f32 = jnp.bfloat16, jnp.float32


def passed_along(value, steps):
    pairs = [(source, (source + steps) % 32) for source in range(32)]
    return lax.ppermute(value, "replica", pairs)


def swapped(value):
    return lax.ppermute(value, "tensor", [(t, t ^ 4) for t in range(8)])


def ring_step(value):
    pairs = []
    for r in range(32):
        way = 1 if r % 2 == 0 else -1
        for t in range(8):
            pairs.append((r * 8 + t, r * 8 + (t & 4) + ((t + way) & 3)))
    return lax.ppermute(value, BOTH, pairs)


def tied(*values):
    return lax.optimization_barrier(values)


def third(own, below, above):
    return (own + below.astype(f32) + above.astype(f32)) / 3.0


def body(context, out_grad, params, momentum):
    r, t = lax.axis_index("replica"), lax.axis_index("tensor")
    h, y = t >> 2, t & 3
    way = 1 - 2 * (r & 1)
    first = h == 0

    own_ctx, cot, mom, param = context[0].T, out_grad[0], momentum[0], params[0]
    tokens = own_ctx.shape[1]

    near, far = own_ctx[:, : tokens // 2], own_ctx[:, tokens // 2 :]
    give_ctx = jnp.where(first, far, near)
    own_half = jnp.where(first, near, far)
    oth_half = swapped(give_ctx)
    cot, give_ctx = tied(cot, give_ctx)

    a0 = cot[:, CUTS[0][0] : CUTS[0][1]]
    b0 = cot[:, CUTS[1][0] : CUTS[1][1]]
    a1 = ring_step(a0)
    param, a0, b0 = tied(param, a0, b0)
    p16 = param.astype(bf16)
    p16, oth_half, a1 = tied(p16, oth_half, a1)
    p_low, p_up = passed_along(p16, 1), passed_along(p16, -1)
    a2 = ring_step(a1)
    b0, a2, a0 = tied(b0, a2, a0)
    p_low, p_up, a2 = tied(p_low, p_up, a2)

    p1 = third(param, p_low, p_up)
    p1_16 = p1.astype(bf16)
    p2_low, p2_up = passed_along(p1_16, 2), passed_along(p1_16, -2)
    a3 = ring_step(a2)
    b1 = ring_step(b0)

    spots = [(y - way * step) & 3 for step in range(4)]

    def in_ring_order(value):
        blocks = [value[:, 256 * k : 256 * k + 256] for k in range(4)]
        return [
            jnp.where(s < 2, jnp.where(s == 0, blocks[0], blocks[1]), jnp.where(s == 2, blocks[2], blocks[3])) for s in spots
        ]

    def gradient(blocks):
        own, oth = None, None
        for step in range(4):
            a = jnp.dot(own_by_step[step], blocks[step], preferred_element_type=f32)
            b = jnp.dot(oth_by_step[step], blocks[step], preferred_element_type=f32)
            own, oth = (a, b) if step == 0 else (own + a, oth + b)
        return own, oth.astype(bf16)

    b2 = ring_step(b1)
    own_by_step, oth_by_step = in_ring_order(own_half), in_ring_order(oth_half)
    own_a, give_a = gradient((a0, a1, a2, a3))
    back_a = swapped(give_a)
    b2, give_a = tied(b2, give_a)
    b3 = ring_step(b2)

    own_b, give_b = gradient((b0, b1, b2, b3))
    back_b = swapped(give_b)
    back_a, p2_low, p2_up, give_b = tied(back_a, p2_low, p2_up, give_b)
    p_mixed = third(p1, p2_low, p2_up)

    v_a = beta_decay * mom[:, CUTS[0][0] : CUTS[0][1]].astype(f32) + own_a + back_a.astype(f32)
    va16 = v_a.astype(bf16)
    va_low, va_up = passed_along(va16, 1), passed_along(va16, -1)
    v_b = beta_decay * mom[:, CUTS[1][0] : CUTS[1][1]].astype(f32) + own_b + back_b.astype(f32)
    vb16 = v_b.astype(bf16)
    vb16, va16 = tied(vb16, va16)
    vb_low, vb_up = passed_along(vb16, 1), passed_along(vb16, -1)

    va_low, va_up, vb16 = tied(va_low, va_up, vb16)
    v1_a = third(v_a, va_low, va_up)
    v1a16 = v1_a.astype(bf16)
    va2_low, va2_up = passed_along(v1a16, 2), passed_along(v1a16, -2)
    vb_low, vb_up, v1a16 = tied(vb_low, vb_up, v1a16)
    v1_b = third(v_b, vb_low, vb_up)
    v1b16 = v1_b.astype(bf16)
    vb2_low, vb2_up = passed_along(v1b16, 2), passed_along(v1b16, -2)

    out_p = p_mixed
    out_m = jnp.zeros(mom.shape, bf16)
    for (lo, hi), v1, low, up in ((CUTS[0], v1_a, va2_low, va2_up), (CUTS[1], v1_b, vb2_low, vb2_up)):
        velocity = third(v1, low, up)
        weights = p_mixed[:, lo:hi] - learn_rate * velocity
        out_p = lax.dynamic_update_slice(out_p, weights, (0, lo))
        out_m = lax.dynamic_update_slice(out_m, velocity.astype(bf16), (0, lo))
    return (out_p[None], out_m[None])


def solution(mesh):
    return jax.shard_map(
        body,
        mesh=mesh,
        in_specs=(
            P("replica", None, "tensor"),
            P("replica", "tensor", None),
            P("replica", "tensor", None),
            P("replica", "tensor", None),
        ),
        out_specs=(P("replica", "tensor", None), P("replica", "tensor", None)),
        check_vma=False,
    )
```

```python
import jax
import jax.numpy as jnp
from jax import lax
from jax.sharding import PartitionSpec as P

learn_rate = 0.01
beta_decay = 0.9

BOTH = ("replica", "tensor")
CUTS = ((0, 2048), (2048, 3584))
bf16, f32 = jnp.bfloat16, jnp.float32


def passed_along(value, steps):
    pairs = [(source, (source + steps) % 32) for source in range(32)]
    return lax.ppermute(value, "replica", pairs)


def swapped(value):
    return lax.ppermute(value, "tensor", [(t, t ^ 4) for t in range(8)])


def ring_step(value):
    pairs = []
    for r in range(32):
        way = 1 if r % 2 == 0 else -1
        for t in range(8):
            pairs.append((r * 8 + t, r * 8 + (t & 4) + ((t + way) & 3)))
    return lax.ppermute(value, BOTH, pairs)


def tied(*values):
    return lax.optimization_barrier(values)


def third(own, below, above):
    return (own + below.astype(f32) + above.astype(f32)) / 3.0


def body(context, out_grad, params, momentum):
    r, t = lax.axis_index("replica"), lax.axis_index("tensor")
    h, y = t >> 2, t & 3
    way = 1 - 2 * (r & 1)
    first = h == 0

    own_ctx, cot, mom, param = context[0].T, out_grad[0], momentum[0], params[0]
    tokens = own_ctx.shape[1]

    p16 = param.astype(bf16)
    p_low, p_up = passed_along(p16, 1), passed_along(p16, -1)

    own_ctx, p16 = tied(own_ctx, p16)
    near, far = own_ctx[:, : tokens // 2], own_ctx[:, tokens // 2 :]
    give_ctx = jnp.where(first, far, near)
    own_half = jnp.where(first, near, far)
    oth_half = swapped(give_ctx)
    cot, give_ctx = tied(cot, give_ctx)

    a0 = cot[:, CUTS[0][0] : CUTS[0][1]]
    b0 = cot[:, CUTS[1][0] : CUTS[1][1]]
    a1 = ring_step(a0)
    b0, a1 = tied(b0, a1)
    b1 = ring_step(b0)
    a2 = ring_step(a1)

    p_low, p_up, a1 = tied(p_low, p_up, a1)
    p1 = third(param, p_low, p_up)
    p1_16 = p1.astype(bf16)
    p1_16, oth_half = tied(p1_16, oth_half)
    p2_low, p2_up = passed_along(p1_16, 2), passed_along(p1_16, -2)
    a2, p1_16 = tied(a2, p1_16)
    a3 = ring_step(a2)

    spots = [(y - way * step) & 3 for step in range(4)]

    def in_ring_order(value):
        blocks = [value[:, 256 * k : 256 * k + 256] for k in range(4)]
        return [
            jnp.where(s < 2, jnp.where(s == 0, blocks[0], blocks[1]), jnp.where(s == 2, blocks[2], blocks[3])) for s in spots
        ]

    def gradient(blocks):
        own, oth = None, None
        for step in range(4):
            a = jnp.dot(own_by_step[step], blocks[step], preferred_element_type=f32)
            b = jnp.dot(oth_by_step[step], blocks[step], preferred_element_type=f32)
            own, oth = (a, b) if step == 0 else (own + a, oth + b)
        return own, oth.astype(bf16)

    b2 = ring_step(b1)
    own_by_step, oth_by_step = in_ring_order(own_half), in_ring_order(oth_half)
    own_a, give_a = gradient((a0, a1, a2, a3))
    back_a = swapped(give_a)
    b2, give_a = tied(b2, give_a)
    b3 = ring_step(b2)

    own_b, give_b = gradient((b0, b1, b2, b3))
    back_b = swapped(give_b)
    back_a, p2_low, p2_up, give_b = tied(back_a, p2_low, p2_up, give_b)
    p_mixed = third(p1, p2_low, p2_up)

    v_a = beta_decay * mom[:, CUTS[0][0] : CUTS[0][1]].astype(f32) + own_a + back_a.astype(f32)
    va16 = v_a.astype(bf16)
    va_low, va_up = passed_along(va16, 1), passed_along(va16, -1)
    v_b = beta_decay * mom[:, CUTS[1][0] : CUTS[1][1]].astype(f32) + own_b + back_b.astype(f32)
    vb16 = v_b.astype(bf16)
    vb16, va16 = tied(vb16, va16)
    vb_low, vb_up = passed_along(vb16, 1), passed_along(vb16, -1)

    va_low, va_up, vb16 = tied(va_low, va_up, vb16)
    v1_a = third(v_a, va_low, va_up)
    v1a16 = v1_a.astype(bf16)
    va2_low, va2_up = passed_along(v1a16, 2), passed_along(v1a16, -2)
    vb_low, vb_up, v1a16 = tied(vb_low, vb_up, v1a16)
    v1_b = third(v_b, vb_low, vb_up)
    v1b16 = v1_b.astype(bf16)
    vb2_low, vb2_up = passed_along(v1b16, 2), passed_along(v1b16, -2)

    out_p = p_mixed
    out_m = jnp.zeros(mom.shape, bf16)
    for (lo, hi), v1, low, up in ((CUTS[0], v1_a, va2_low, va2_up), (CUTS[1], v1_b, vb2_low, vb2_up)):
        velocity = third(v1, low, up)
        weights = p_mixed[:, lo:hi] - learn_rate * velocity
        out_p = lax.dynamic_update_slice(out_p, weights, (0, lo))
        out_m = lax.dynamic_update_slice(out_m, velocity.astype(bf16), (0, lo))
    return (out_p[None], out_m[None])


def solution(mesh):
    return jax.shard_map(
        body,
        mesh=mesh,
        in_specs=(
            P("replica", None, "tensor"),
            P("replica", "tensor", None),
            P("replica", "tensor", None),
            P("replica", "tensor", None),
        ),
        out_specs=(P("replica", "tensor", None), P("replica", "tensor", None)),
        check_vma=False,
    )
```

```python
import jax
import jax.numpy as jnp
from jax import lax
from jax.sharding import PartitionSpec as P

learn_rate = 0.01
beta_decay = 0.9

BOTH = ("replica", "tensor")
CUTS = ((0, 2048), (2048, 3584))
bf16, f32 = jnp.bfloat16, jnp.float32


def passed_along(value, steps):
    pairs = [(source, (source + steps) % 32) for source in range(32)]
    return lax.ppermute(value, "replica", pairs)


def swapped(value):
    return lax.ppermute(value, "tensor", [(t, t ^ 4) for t in range(8)])


def ring_step(value):
    pairs = []
    for r in range(32):
        way = 1 if r % 2 == 0 else -1
        for t in range(8):
            pairs.append((r * 8 + t, r * 8 + (t & 4) + ((t + way) & 3)))
    return lax.ppermute(value, BOTH, pairs)


def tied(*values):
    return lax.optimization_barrier(values)


def third(own, below, above):
    return (own + below.astype(f32) + above.astype(f32)) / 3.0


def body(context, out_grad, params, momentum):
    r, t = lax.axis_index("replica"), lax.axis_index("tensor")
    h, y = t >> 2, t & 3
    way = 1 - 2 * (r & 1)
    first = h == 0

    own_ctx, cot, mom, param = context[0].T, out_grad[0], momentum[0], params[0]
    tokens = own_ctx.shape[1]

    p16 = param.astype(bf16)
    p_low, p_up = passed_along(p16, 1), passed_along(p16, -1)

    own_ctx, p16 = tied(own_ctx, p16)
    near, far = own_ctx[:, : tokens // 2], own_ctx[:, tokens // 2 :]
    give_ctx = jnp.where(first, far, near)
    own_half = jnp.where(first, near, far)
    oth_half = swapped(give_ctx)
    cot, give_ctx = tied(cot, give_ctx)

    a0 = cot[:, CUTS[0][0] : CUTS[0][1]]
    b0 = cot[:, CUTS[1][0] : CUTS[1][1]]
    a1 = ring_step(a0)
    b0, a1 = tied(b0, a1)
    b1 = ring_step(b0)
    a2 = ring_step(a1)

    p_low, p_up, a1 = tied(p_low, p_up, a1)
    p1 = third(param, p_low, p_up)
    p1_16 = p1.astype(bf16)
    p1_16, oth_half = tied(p1_16, oth_half)
    p2_low, p2_up = passed_along(p1_16, 2), passed_along(p1_16, -2)
    a2, p1_16 = tied(a2, p1_16)
    a3 = ring_step(a2)

    spots = [(y - way * step) & 3 for step in range(4)]

    def in_ring_order(value):
        blocks = [value[:, 256 * k : 256 * k + 256] for k in range(4)]
        return [
            jnp.where(s < 2, jnp.where(s == 0, blocks[0], blocks[1]), jnp.where(s == 2, blocks[2], blocks[3])) for s in spots
        ]

    def gradient(blocks):
        own, oth = None, None
        for step in range(4):
            a = jnp.dot(own_by_step[step], blocks[step], preferred_element_type=f32)
            b = jnp.dot(oth_by_step[step], blocks[step], preferred_element_type=f32)
            own, oth = (a, b) if step == 0 else (own + a, oth + b)
        return own, oth.astype(bf16)

    b2 = ring_step(b1)
    own_by_step, oth_by_step = in_ring_order(own_half), in_ring_order(oth_half)
    own_a, give_a = gradient((a0, a1, a2, a3))
    back_a = swapped(give_a)
    b2, give_a = tied(b2, give_a)
    b3 = ring_step(b2)

    own_b, give_b = gradient((b0, b1, b2, b3))
    back_b = swapped(give_b)
    back_a, p2_low, p2_up, give_b = tied(back_a, p2_low, p2_up, give_b)
    p_mixed = third(p1, p2_low, p2_up)

    v_a = beta_decay * mom[:, CUTS[0][0] : CUTS[0][1]].astype(f32) + own_a + back_a.astype(f32)
    va16 = v_a.astype(bf16)
    va_low, va_up = passed_along(va16, 1), passed_along(va16, -1)
    v_b = beta_decay * mom[:, CUTS[1][0] : CUTS[1][1]].astype(f32) + own_b + back_b.astype(f32)
    vb16 = v_b.astype(bf16)
    vb16, va16 = tied(vb16, va16)
    vb_low, vb_up = passed_along(vb16, 1), passed_along(vb16, -1)

    va_low, va_up, vb16 = tied(va_low, va_up, vb16)
    v1_a = third(v_a, va_low, va_up)
    v1a16 = v1_a.astype(bf16)
    va2_low, va2_up = passed_along(v1a16, 2), passed_along(v1a16, -2)
    vb_low, vb_up, v1a16 = tied(vb_low, vb_up, v1a16)
    v1_b = third(v_b, vb_low, vb_up)
    v1b16 = v1_b.astype(bf16)
    vb2_low, vb2_up = passed_along(v1b16, 2), passed_along(v1b16, -2)

    momentum_a = third(v1_a, va2_low, va2_up)
    momentum_b = third(v1_b, vb2_low, vb2_up)
    out_p = p_mixed
    for (lo, hi), velocity in ((CUTS[0], momentum_a), (CUTS[1], momentum_b)):
        out_p = lax.dynamic_update_slice(out_p, p_mixed[:, lo:hi] - learn_rate * velocity, (0, lo))
    out_p, vb2_low, vb2_up = tied(out_p, vb2_low, vb2_up)
    last = third(v1_b, vb2_low, vb2_up)
    out_m = jnp.concatenate([momentum_a.astype(bf16), last.astype(bf16)], 1)
    return (out_p[None], out_m[None])


def solution(mesh):
    return jax.shard_map(
        body,
        mesh=mesh,
        in_specs=(
            P("replica", None, "tensor"),
            P("replica", "tensor", None),
            P("replica", "tensor", None),
            P("replica", "tensor", None),
        ),
        out_specs=(P("replica", "tensor", None), P("replica", "tensor", None)),
        check_vma=False,
    )
```
